512 devices in a mesh: replica: 8 (over z_lo, core), fsdp: 64 (over z_hi, y, x).
Axes of the slice: x: 4, y: 4, z: 16 (z_hi: 4, z_lo: 4; z = z_hi * 4 + z_lo), core: 2. Of those that a mesh axis runs over, the one named last changes fastest.
Arguments:
- hidden: bfloat16 [65536, 8192], P(('replica', 'fsdp')), may hold values from -6 to 6
- key_cotangent: bfloat16 [65536, 512], P(('replica', 'fsdp')), may hold values from -0.15625 to 0.15625
- key_weight: float32 [8, 8192, 512], P('replica', 'fsdp'), may hold values from -0.0625 to 0.0625
- first_moment: float32 [8, 8192, 512], P('replica', 'fsdp'), may hold values from -4 to 4
- second_moment: float32 [8, 8192, 512], P('replica', 'fsdp'), may hold values from 0.01 to 1
- step_index: int32 [], replicated, may hold values from 1 to 1000
- anchor: float32 [8192, 512], P('fsdp'), may hold values from -6 to 6
- outer_momentum: float32 [8192, 512], P('fsdp'), may hold values from -6 to 6
- replica_fragment: bfloat16 [8, 8192, 512], P('replica', 'fsdp'), may hold values from -6 to 6
Outputs:
- new_weight: float32 [8, 8192, 512], P('replica', 'fsdp')
- new_first: float32 [8, 8192, 512], P('replica', 'fsdp')
- new_second: float32 [8, 8192, 512], P('replica', 'fsdp')
- new_anchor: float32 [8192, 512], P('fsdp')
- new_momentum: float32 [8192, 512], P('fsdp')
The draws below stay inside these ranges and needn't reach their ends.
All inputs are finite; a program needn't handle non-finite values.
Results may differ from the reference program's by a relative error of at most 0.0003.
Values may be sent and summed in bfloat16 or wider, within the bound.
A program may use at most 64 MiB of HBM per device.

```python
import math
import jax
import jax.numpy as jnp
from jax import lax

D = 8192
KW = 512
TOKENS = 65536
N_REPLICA = 8


def level_of(key, dims, split, least, top_value):
    gain, own = 1.0, jax.random.fold_in(key, 6)
    for axis_at, blocks in split:
        steps = jnp.exp(jax.random.uniform(jax.random.fold_in(own, axis_at), (blocks,), jnp.float32, least / len(split), top_value / len(split)))
        gain = gain * jnp.repeat(steps, dims[axis_at] // blocks).reshape([-1 if axis == axis_at else 1 for axis in range(len(dims))])
    return gain


def gaussian(stream_key, extent, width, limit, shards=(), kind=jnp.bfloat16):
    drawn = width * jax.random.normal(stream_key, extent, jnp.float32)
    if shards:
        drawn = drawn * level_of(stream_key, extent, shards, -0.22, 0.18)
    return jnp.clip(drawn, -limit, limit).astype(kind)


def setup_inputs(seed: int = 0) -> dict:
    seeds = jax.random.split(jax.random.key(seed), 10)
    return {
        "hidden": gaussian(seeds[0], (TOKENS, D), 1.0, 6.0, ((0, 512),)),
        "key_cotangent": gaussian(seeds[1], (TOKENS, KW), 0.01, 0.15625, ((0, 512),)),
        "key_weight": gaussian(seeds[2], (N_REPLICA, D, KW), D ** -0.5, 0.0625, ((0, 8), (1, 64)), jnp.float32),
        "first_moment": gaussian(seeds[3], (N_REPLICA, D, KW), 0.3, 4.0, ((0, 8), (1, 64)), jnp.float32),
        "second_moment": jnp.clip(jnp.exp(math.log(1.0) - 4.6051702 * jax.random.uniform(seeds[4], (N_REPLICA, D, KW), jnp.float32) ** level_of(seeds[4], (N_REPLICA, D, KW), ((0, 8), (1, 64)), -0.2, 0.2)), 0.01, 1.0),
        "step_index": jax.random.randint(seeds[5], (), 1, 1001).astype(jnp.int32),
        "anchor": gaussian(seeds[6], (D, KW), 1.0, 6.0, ((0, 64),), jnp.float32),
        "outer_momentum": gaussian(seeds[7], (D, KW), 0.5, 6.0, ((0, 64),), jnp.float32),
        "replica_fragment": gaussian(seeds[8], (N_REPLICA, D, KW), 1.0, 6.0, ((0, 8), (1, 64))),
    }


def reference(hidden, key_cotangent, key_weight, first_moment, second_moment, step_index, anchor, outer_momentum, replica_fragment):
    per = hidden.shape[0] // N_REPLICA
    inputs = hidden.reshape(N_REPLICA, per, hidden.shape[1])
    cotans = key_cotangent.reshape(N_REPLICA, per, key_cotangent.shape[1])

    def one(pair):
        return lax.dot_general(pair[0], pair[1], (((0,), (0,)), ((), ())), preferred_element_type=jnp.float32)
    grad = lax.map(one, (inputs, cotans))
    new_first = 0.9 * first_moment + 0.1 * grad
    new_second = 0.999 * second_moment + 0.001 * grad * grad
    steps = step_index.astype(jnp.float32)
    corr_one = 1.0 - jnp.power(jnp.float32(0.9), steps)
    corr_two = 1.0 - jnp.power(jnp.float32(0.999), steps)
    update = new_first / corr_one / (jnp.sqrt(new_second / corr_two) + 1e-08)
    new_weight = key_weight - 0.01 * (update + 0.1 * key_weight)
    differ = anchor[None] - replica_fragment.astype(jnp.float32)
    delta = lax.optimization_barrier(jnp.sum(differ, axis=0)) / N_REPLICA
    new_momentum = 0.9 * outer_momentum + delta
    new_anchor = anchor - 0.7 * (delta + 0.9 * new_momentum)
    return (new_weight, new_first, new_second, new_anchor, new_momentum)
```

```python
import functools

import jax
import jax.numpy as jnp
from jax import lax
from jax.experimental import pallas as pl
from jax.experimental.pallas import tpu as pltpu
from jax.sharding import PartitionSpec as P

MESH = pl.DeviceIdType.MESH
STEPS = (2, 1, 3, 0)


def exchange(
    hidden, cotan, frag, anchor, grad, delta,
    hbuf, cbuf, part, relay, fin, dpart, danchor, dsum,
    local, hsend, hrecv, csend, crecv, zsend, zrecv, dsend, drecv,
):
    rep = lax.axis_index("replica")
    row = lax.axis_index("fsdp")
    zh, y, x = row // 16, (row // 4) % 4, row % 4

    def plane(dy, dx):
        return (rep, zh * 16 + ((y + dy) % 4) * 4 + (x + dx) % 4)

    def along_z(dz):
        return (rep, ((zh + dz) % 4) * 16 + y * 4 + x)

    def other(j):
        return ((rep + j) % 8, row)

    def send(src, dst, ssem, rsem, device):
        pltpu.make_async_remote_copy(
            src_ref=src, dst_ref=dst, send_sem=ssem, recv_sem=rsem, device_id=device, device_id_type=MESH
        ).start()

    def wait(ref, sem):
        pltpu.make_async_copy(ref, ref, sem).wait()

    barrier = pltpu.get_barrier_semaphore()

    @pl.loop(1, 16)
    def _(k):
        pl.semaphore_signal(barrier, inc=1, device_id=plane(k // 4, k % 4), device_id_type=MESH)

    @pl.loop(1, 8)
    def _(j):
        pl.semaphore_signal(barrier, inc=1, device_id=other(j), device_id_type=MESH)

    for dz in (1, 3):
        pl.semaphore_signal(barrier, inc=1, device_id=along_z(dz), device_id_type=MESH)

    def column(q, dy, dx):
        start = ((zh + STEPS[q]) % 4) * 16 + ((y + dy) % 4) * 4 + (x + dx) % 4
        return pl.ds(pl.multiple_of(start * 128, 128), 128)

    mine = pl.ds(pl.multiple_of(rep * 16, 16), 16)
    own = [pltpu.make_async_copy(cotan, cbuf.at[0, 0], local.at[0])]
    own += [
        pltpu.make_async_copy(hidden.at[:, column(q, 0, 0)], hbuf.at[q, pl.ds(0, 128)], local.at[1 + q])
        for q in range(4)
    ]
    own += [
        pltpu.make_async_copy(frag.at[0, mine], dpart.at[0], local.at[5]),
        pltpu.make_async_copy(anchor.at[mine], danchor, local.at[6]),
    ]
    for copy in own:
        copy.start()
    pl.semaphore_wait(barrier, 24)

    for d in (1, 3, 2):
        send(cotan.at[pl.ds(0, 64)], cbuf.at[0, d, pl.ds(0, 64)], csend.at[0], crecv.at[0], plane(0, d))
        send(cotan.at[pl.ds(64, 64)], cbuf.at[d, 0, pl.ds(64, 64)], csend.at[1], crecv.at[1], plane(d, 0))

    @pl.loop(1, 8)
    def _(j):
        rows = pl.ds(pl.multiple_of(((rep + j) % 8) * 16, 16), 16)
        send(frag.at[0, rows], dpart.at[j], dsend.at[0], drecv.at[0], other(j))

    def features(q):
        @pl.loop(1, 16)
        def _(k):
            dy, dx = k // 4, k % 4
            send(
                hidden.at[:, column(q, dy, dx)],
                hbuf.at[q, pl.ds(pl.multiple_of(k * 128, 128), 128)],
                hsend.at[q], hrecv.at[q], plane(dy, dx),
            )

    features(0)
    own[0].wait()
    wait(cbuf.at[0, pl.ds(1, 3), pl.ds(0, 64)], crecv.at[0])
    for d in (1, 3, 2):
        send(cbuf.at[0, :, pl.ds(0, 64)], cbuf.at[d, :, pl.ds(0, 64)], csend.at[2], crecv.at[2], plane(d, 0))
    wait(cbuf.at[pl.ds(1, 3), 0, pl.ds(64, 64)], crecv.at[1])
    for d in (1, 3, 2):
        send(cbuf.at[:, 0, pl.ds(64, 64)], cbuf.at[:, d, pl.ds(64, 64)], csend.at[3], crecv.at[3], plane(0, d))
    features(1)
    features(2)
    features(3)

    for copy in own[5:]:
        copy.wait()
    wait(dpart.at[pl.ds(1, 7)], drecv.at[0])
    total = danchor[...] - dpart[0].astype(jnp.float32)
    for j in range(1, 8):
        total += danchor[...] - dpart[j].astype(jnp.float32)
    dsum[mine] = total / 8

    @pl.loop(1, 8)
    def _(j):
        send(dsum.at[mine], dsum.at[mine], dsend.at[1], drecv.at[1], other(j))

    wait(cbuf.at[pl.ds(1, 3), :, pl.ds(0, 64)], crecv.at[2])
    wait(cbuf.at[:, pl.ds(1, 3), pl.ds(64, 64)], crecv.at[3])

    def product(q):
        own[1 + q].wait()
        wait(hbuf.at[q, pl.ds(128, 1920)], hrecv.at[q])
        left = hbuf[q]
        for half in range(2):
            right = cbuf[:, :, :, pl.ds(half * 256, 256)].reshape(2048, 256)
            part[q, half] = lax.dot_general(
                left, right, (((0,), (0,)), ((), ())), preferred_element_type=jnp.float32
            )

    product(0)
    send(part.at[0, 0], relay.at[0], zsend.at[0], zrecv.at[0], along_z(1))
    send(part.at[0, 1], relay.at[1], zsend.at[1], zrecv.at[1], along_z(3))
    product(1)
    send(part.at[1, 1], fin.at[1], zsend.at[2], zrecv.at[2], along_z(1))
    product(2)
    send(part.at[2, 0], fin.at[2], zsend.at[3], zrecv.at[3], along_z(3))
    wait(relay.at[0], zrecv.at[0])
    part[1, 0] += relay[0]
    send(part.at[1, 0], fin.at[0], zsend.at[4], zrecv.at[4], along_z(1))
    wait(relay.at[1], zrecv.at[1])
    part[2, 1] += relay[1]
    send(part.at[2, 1], fin.at[3], zsend.at[5], zrecv.at[5], along_z(3))
    product(3)

    wait(dsum.at[pl.ds(0, 112)], drecv.at[1])
    delta[...] = dsum[...]
    wait(fin.at[1], zrecv.at[2])
    wait(fin.at[2], zrecv.at[3])
    wait(fin.at[0], zrecv.at[4])
    grad[:, pl.ds(0, 256)] = part[3, 0] + fin[0] + fin[2]
    wait(fin.at[3], zrecv.at[5])
    grad[:, pl.ds(256, 256)] = part[3, 1] + fin[1] + fin[3]

    for q in range(4):
        wait(hbuf.at[q, pl.ds(128, 1920)], hsend.at[q])
    wait(cbuf.at[0, pl.ds(1, 3), pl.ds(0, 64)], csend.at[0])
    wait(cbuf.at[pl.ds(1, 3), 0, pl.ds(64, 64)], csend.at[1])
    wait(cbuf.at[pl.ds(1, 3), :, pl.ds(0, 64)], csend.at[2])
    wait(cbuf.at[:, pl.ds(1, 3), pl.ds(64, 64)], csend.at[3])
    for m in range(6):
        wait(relay.at[0], zsend.at[m])
    wait(dpart.at[pl.ds(1, 7)], dsend.at[0])
    wait(dsum.at[pl.ds(0, 112)], dsend.at[1])


def body(
    hidden,
    key_cotangent,
    key_weight,
    first_moment,
    second_moment,
    step_index,
    anchor,
    outer_momentum,
    replica_fragment,
):
    dma = pltpu.SemaphoreType.DMA
    grad, delta = pl.pallas_call(
        exchange,
        out_shape=[jax.ShapeDtypeStruct((128, 512), jnp.float32)] * 2,
        in_specs=[pl.BlockSpec(memory_space=pl.ANY)] * 4,
        out_specs=[pl.BlockSpec(memory_space=pltpu.VMEM)] * 2,
        scratch_shapes=[
            pltpu.VMEM((4, 2048, 128), jnp.bfloat16),
            pltpu.VMEM((4, 4, 128, 512), jnp.bfloat16),
            pltpu.VMEM((4, 2, 128, 256), jnp.float32),
            pltpu.VMEM((2, 128, 256), jnp.float32),
            pltpu.VMEM((4, 128, 256), jnp.float32),
            pltpu.VMEM((8, 16, 512), jnp.bfloat16),
            pltpu.VMEM((16, 512), jnp.float32),
            pltpu.VMEM((128, 512), jnp.float32),
            dma((7,)), dma((4,)), dma((4,)), dma((4,)), dma((4,)), dma((6,)), dma((6,)), dma((2,)), dma((2,)),
        ],
        compiler_params=pltpu.CompilerParams(
            collective_id=0, has_side_effects=True, vmem_limit_bytes=40 * 1024 * 1024
        ),
        cost_estimate=pl.CostEstimate(flops=2 * 2048 * 512 * 512, bytes_accessed=8 << 20, transcendentals=0),
        name="exchange",
    )(hidden, key_cotangent, replica_fragment, anchor)
    grad = grad[None]
    new_first = 0.9 * first_moment + 0.1 * grad
    new_second = 0.999 * second_moment + 0.001 * grad * grad
    steps = step_index.astype(jnp.float32)
    corr_one = 1.0 - jnp.power(jnp.float32(0.9), steps)
    corr_two = 1.0 - jnp.power(jnp.float32(0.999), steps)
    update = new_first / corr_one / (jnp.sqrt(new_second / corr_two) + 1e-08)
    new_weight = key_weight - 0.01 * (update + 0.1 * key_weight)
    new_momentum = 0.9 * outer_momentum + delta
    new_anchor = anchor - 0.7 * (delta + 0.9 * new_momentum)
    return (new_weight, new_first, new_second, new_anchor, new_momentum)


def solution(mesh):
    return jax.shard_map(
        body,
        mesh=mesh,
        in_specs=(
            P(("replica", "fsdp"), None),
            P(("replica", "fsdp"), None),
            P("replica", "fsdp", None),
            P("replica", "fsdp", None),
            P("replica", "fsdp", None),
            P(),
            P("fsdp", None),
            P("fsdp", None),
            P("replica", "fsdp", None),
        ),
        out_specs=(
            P("replica", "fsdp", None),
            P("replica", "fsdp", None),
            P("replica", "fsdp", None),
            P("fsdp", None),
            P("fsdp", None),
        ),
        check_vma=False,
    )
```

```python
import functools

import jax
import jax.numpy as jnp
from jax import lax
from jax.experimental import pallas as pl
from jax.experimental.pallas import tpu as pltpu
from jax.sharding import PartitionSpec as P

MESH = pl.DeviceIdType.MESH
STEPS = (2, 1, 3, 0)


def exchange(
    hidden, cotan, frag, anchor, grad, delta,
    hbuf, cbuf, part, code, gain, recode, regain, dpart, danchor, dsum,
    local, hsend, hrecv, csend, crecv, zsend, zrecv, dsend, drecv, ready,
):
    rep = lax.axis_index("replica")
    row = lax.axis_index("fsdp")
    zh, y, x = row // 16, (row // 4) % 4, row % 4

    def plane(dy, dx):
        return (rep, zh * 16 + ((y + dy) % 4) * 4 + (x + dx) % 4)

    def along_z(dz):
        return (rep, ((zh + dz) % 4) * 16 + y * 4 + x)

    def other(j):
        return ((rep + j) % 8, row)

    def send(src, dst, ssem, rsem, device):
        pltpu.make_async_remote_copy(
            src_ref=src, dst_ref=dst, send_sem=ssem, recv_sem=rsem, device_id=device, device_id_type=MESH
        ).start()

    def wait(ref, sem):
        pltpu.make_async_copy(ref, ref, sem).wait()

    up, down = (zh + 1) % 4, (zh + 3) % 4
    barrier = pltpu.get_barrier_semaphore()

    @pl.loop(1, 16)
    def _(k):
        pl.semaphore_signal(barrier, inc=1, device_id=plane(k // 4, k % 4), device_id_type=MESH)

    @pl.loop(rep + 1, 8)
    def _(r):
        pl.semaphore_signal(barrier, inc=1, device_id=(r, row), device_id_type=MESH)

    for dz, at in ((1, up), (3, down)):
        @pl.when(at > zh)
        def _():
            pl.semaphore_signal(barrier, inc=1, device_id=along_z(dz), device_id_type=MESH)

    lower = (up < zh).astype(jnp.int32) + (down < zh).astype(jnp.int32)

    def column(q, dy, dx):
        start = ((zh + STEPS[q]) % 4) * 16 + ((y + dy) % 4) * 4 + (x + dx) % 4
        return pl.ds(pl.multiple_of(start * 128, 128), 128)

    mine = pl.ds(pl.multiple_of(rep * 16, 16), 16)
    own = [pltpu.make_async_copy(cotan, cbuf.at[0, 0], local.at[0])]
    own += [
        pltpu.make_async_copy(hidden.at[:, column(q, 0, 0)], hbuf.at[q, pl.ds(0, 128)], local.at[1 + q])
        for q in range(4)
    ]
    own += [
        pltpu.make_async_copy(frag.at[0, mine], dpart.at[0], local.at[5]),
        pltpu.make_async_copy(anchor.at[mine], danchor, local.at[6]),
    ]
    for copy in own:
        copy.start()
    pl.semaphore_wait(barrier, 15 + rep + lower)

    @pl.loop(0, rep)
    def _(r):
        pl.semaphore_signal(ready.at[0], inc=1, device_id=(r, row), device_id_type=MESH)

    for dz, at in ((1, up), (3, down)):
        @pl.when(at < zh)
        def _():
            pl.semaphore_signal(ready.at[1], inc=1, device_id=along_z(dz), device_id_type=MESH)

    for d in (1, 3, 2):
        send(cotan.at[pl.ds(0, 64)], cbuf.at[0, d, pl.ds(0, 64)], csend.at[0], crecv.at[0], plane(0, d))
        send(cotan.at[pl.ds(64, 64)], cbuf.at[d, 0, pl.ds(64, 64)], csend.at[1], crecv.at[1], plane(d, 0))

    def features(q):
        @pl.loop(1, 16)
        def _(k):
            dy, dx = k // 4, k % 4
            send(
                hidden.at[:, column(q, dy, dx)],
                hbuf.at[q, pl.ds(pl.multiple_of(k * 128, 128), 128)],
                hsend.at[q], hrecv.at[q], plane(dy, dx),
            )

    features(0)

    @pl.when(rep < 7)
    def _():
        pl.semaphore_wait(ready.at[0], 7 - rep)

    @pl.loop(1, 8)
    def _(j):
        rows = pl.ds(pl.multiple_of(((rep + j) % 8) * 16, 16), 16)
        send(frag.at[0, rows], dpart.at[j], dsend.at[0], drecv.at[0], other(j))

    own[0].wait()
    wait(cbuf.at[0, pl.ds(1, 3), pl.ds(0, 64)], crecv.at[0])
    for d in (1, 3, 2):
        send(cbuf.at[0, :, pl.ds(0, 64)], cbuf.at[d, :, pl.ds(0, 64)], csend.at[2], crecv.at[2], plane(d, 0))
    wait(cbuf.at[pl.ds(1, 3), 0, pl.ds(64, 64)], crecv.at[1])
    for d in (1, 3, 2):
        send(cbuf.at[:, 0, pl.ds(64, 64)], cbuf.at[:, d, pl.ds(64, 64)], csend.at[3], crecv.at[3], plane(0, d))
    own[1].wait()
    wait(hbuf.at[0, pl.ds(128, 1920)], hrecv.at[0])
    features(1)

    for copy in own[5:]:
        copy.wait()
    wait(dpart.at[pl.ds(1, 7)], drecv.at[0])
    total = danchor[...] - dpart[0].astype(jnp.float32)
    for j in range(1, 8):
        total += danchor[...] - dpart[j].astype(jnp.float32)
    dsum[mine] = total / 8

    for j in (2, 4, 6):
        send(dsum.at[mine], dsum.at[mine], dsend.at[1], drecv.at[1], other(j))
    sibling = (rep + 1 - 2 * (rep % 2), row)
    send(dsum.at[mine], dsum.at[mine], dsend.at[2], drecv.at[2], sibling)

    wait(cbuf.at[pl.ds(1, 3), :, pl.ds(0, 64)], crecv.at[2])
    wait(cbuf.at[:, pl.ds(1, 3), pl.ds(64, 64)], crecv.at[3])

    def product(q):
        if q:
            own[1 + q].wait()
            wait(hbuf.at[q, pl.ds(128, 1920)], hrecv.at[q])
        if q < 2:
            features(q + 2)
        left = hbuf[q]
        for half in range(2):
            right = cbuf[:, :, :, pl.ds(half * 256, 256)].reshape(2048, 256)
            part[q, half] = lax.dot_general(
                left, right, (((0,), (0,)), ((), ())), preferred_element_type=jnp.float32
            )

    def pass_on(m, value, dz):
        top = jnp.maximum(jnp.max(jnp.abs(value), axis=0, keepdims=True), 1e-30)
        code[m] = jnp.round(value * (32767.0 / top)).astype(jnp.int32).astype(jnp.int16)
        gain[m] = jnp.broadcast_to(top, (8, 256))
        send(code.at[m], recode.at[m], zsend.at[m], zrecv.at[m], along_z(dz))
        send(gain.at[m], regain.at[m], zsend.at[6 + m], zrecv.at[6 + m], along_z(dz))

    def received(m):
        wait(recode.at[m], zrecv.at[m])
        wait(regain.at[m], zrecv.at[6 + m])
        return recode[m].astype(jnp.int32).astype(jnp.float32) * (regain[m, 0:1] * (1.0 / 32767.0))

    product(0)
    @pl.when(lower < 2)
    def _():
        pl.semaphore_wait(ready.at[1], 2 - lower)

    pass_on(0, part[0, 0], 1)
    pass_on(1, part[0, 1], 3)
    product(1)
    pass_on(2, part[1, 1], 1)
    product(2)
    pass_on(3, part[2, 0], 3)
    wait(dsum.at[pl.ds(0, 48)], drecv.at[1])
    for j in (2, 4, 6):
        there = pl.ds(pl.multiple_of(((rep + j) % 8) * 16, 16), 16)
        send(dsum.at[there], dsum.at[there], dsend.at[3], drecv.at[3], sibling)
    pass_on(4, part[1, 0] + received(0), 1)
    pass_on(5, part[2, 1] + received(1), 3)
    product(3)

    wait(dsum.at[pl.ds(0, 16)], drecv.at[2])
    wait(dsum.at[pl.ds(0, 48)], drecv.at[3])
    delta[...] = dsum[...]
    part[3, 1] += received(2)
    part[3, 0] += received(3)
    grad[:, pl.ds(0, 256)] = part[3, 0] + received(4)
    grad[:, pl.ds(256, 256)] = part[3, 1] + received(5)

    for q in range(4):
        wait(hbuf.at[q, pl.ds(128, 1920)], hsend.at[q])
    wait(cbuf.at[0, pl.ds(1, 3), pl.ds(0, 64)], csend.at[0])
    wait(cbuf.at[pl.ds(1, 3), 0, pl.ds(64, 64)], csend.at[1])
    wait(cbuf.at[pl.ds(1, 3), :, pl.ds(0, 64)], csend.at[2])
    wait(cbuf.at[:, pl.ds(1, 3), pl.ds(64, 64)], csend.at[3])
    for m in range(6):
        wait(code.at[m], zsend.at[m])
        wait(gain.at[m], zsend.at[6 + m])
    wait(dpart.at[pl.ds(1, 7)], dsend.at[0])
    wait(dsum.at[pl.ds(0, 48)], dsend.at[1])
    wait(dsum.at[pl.ds(0, 16)], dsend.at[2])
    wait(dsum.at[pl.ds(0, 48)], dsend.at[3])


def body(
    hidden,
    key_cotangent,
    key_weight,
    first_moment,
    second_moment,
    step_index,
    anchor,
    outer_momentum,
    replica_fragment,
):
    dma = pltpu.SemaphoreType.DMA
    grad, delta = pl.pallas_call(
        exchange,
        out_shape=[jax.ShapeDtypeStruct((128, 512), jnp.float32)] * 2,
        in_specs=[pl.BlockSpec(memory_space=pl.ANY)] * 4,
        out_specs=[pl.BlockSpec(memory_space=pltpu.VMEM)] * 2,
        scratch_shapes=[
            pltpu.VMEM((4, 2048, 128), jnp.bfloat16),
            pltpu.VMEM((4, 4, 128, 512), jnp.bfloat16),
            pltpu.VMEM((4, 2, 128, 256), jnp.float32),
            pltpu.VMEM((6, 128, 256), jnp.int16),
            pltpu.VMEM((6, 8, 256), jnp.float32),
            pltpu.VMEM((6, 128, 256), jnp.int16),
            pltpu.VMEM((6, 8, 256), jnp.float32),
            pltpu.VMEM((8, 16, 512), jnp.bfloat16),
            pltpu.VMEM((16, 512), jnp.float32),
            pltpu.VMEM((128, 512), jnp.float32),
            dma((7,)), dma((4,)), dma((4,)), dma((4,)), dma((4,)), dma((12,)), dma((12,)), dma((4,)), dma((4,)),
            pltpu.SemaphoreType.REGULAR((2,)),
        ],
        compiler_params=pltpu.CompilerParams(
            collective_id=0, has_side_effects=True, vmem_limit_bytes=60 * 1024 * 1024
        ),
        cost_estimate=pl.CostEstimate(flops=2 * 2048 * 512 * 512, bytes_accessed=8 << 20, transcendentals=0),
        name="exchange",
    )(hidden, key_cotangent, replica_fragment, anchor)
    grad = grad[None]
    new_first = 0.9 * first_moment + 0.1 * grad
    new_second = 0.999 * second_moment + 0.001 * grad * grad
    steps = step_index.astype(jnp.float32)
    corr_one = 1.0 - jnp.power(jnp.float32(0.9), steps)
    corr_two = 1.0 - jnp.power(jnp.float32(0.999), steps)
    update = new_first / corr_one / (jnp.sqrt(new_second / corr_two) + 1e-08)
    new_weight = key_weight - 0.01 * (update + 0.1 * key_weight)
    new_momentum = 0.9 * outer_momentum + delta
    new_anchor = anchor - 0.7 * (delta + 0.9 * new_momentum)
    return (new_weight, new_first, new_second, new_anchor, new_momentum)


def solution(mesh):
    return jax.shard_map(
        body,
        mesh=mesh,
        in_specs=(
            P(("replica", "fsdp"), None),
            P(("replica", "fsdp"), None),
            P("replica", "fsdp", None),
            P("replica", "fsdp", None),
            P("replica", "fsdp", None),
            P(),
            P("fsdp", None),
            P("fsdp", None),
            P("replica", "fsdp", None),
        ),
        out_specs=(
            P("replica", "fsdp", None),
            P("replica", "fsdp", None),
            P("replica", "fsdp", None),
            P("fsdp", None),
            P("fsdp", None),
        ),
        check_vma=False,
    )
```

```python
import functools

import jax
import jax.numpy as jnp
from jax import lax
from jax.experimental import pallas as pl
from jax.experimental.pallas import tpu as pltpu
from jax.sharding import PartitionSpec as P

MESH = pl.DeviceIdType.MESH
STEPS = (2, 1, 3, 0)
BY_X = (True, False, False, True)


def exchange(
    hidden, cotan, frag, anchor, grad, delta,
    hbuf, cbuf, ycode, ygain, yrecode, yregain, part, code, gain, recode, regain, dpart, danchor, dsum,
    local, hsend, hrecv, csend, crecv, ysend, yrecv, zsend, zrecv, dsend, drecv, ready,
):
    rep = lax.axis_index("replica")
    row = lax.axis_index("fsdp")
    zh, y, x = row // 16, (row // 4) % 4, row % 4

    def along_x(dx):
        return (rep, zh * 16 + y * 4 + (x + dx) % 4)

    def along_y(dy):
        return (rep, zh * 16 + ((y + dy) % 4) * 4 + x)

    def along_z(dz):
        return (rep, ((zh + dz) % 4) * 16 + y * 4 + x)

    def other(j):
        return ((rep + j) % 8, row)

    def send(src, dst, ssem, rsem, device):
        pltpu.make_async_remote_copy(
            src_ref=src, dst_ref=dst, send_sem=ssem, recv_sem=rsem, device_id=device, device_id_type=MESH
        ).start()

    def wait(ref, sem):
        pltpu.make_async_copy(ref, ref, sem).wait()

    up, down = (zh + 1) % 4, (zh + 3) % 4
    barrier = pltpu.get_barrier_semaphore()
    for d in (1, 2, 3):
        pl.semaphore_signal(barrier, inc=1, device_id=along_x(d), device_id_type=MESH)
        pl.semaphore_signal(barrier, inc=1, device_id=along_y(d), device_id_type=MESH)

    @pl.loop(rep + 1, 8)
    def _(r):
        pl.semaphore_signal(barrier, inc=1, device_id=(r, row), device_id_type=MESH)

    for dz, at in ((1, up), (3, down)):
        @pl.when(at > zh)
        def _():
            pl.semaphore_signal(barrier, inc=1, device_id=along_z(dz), device_id_type=MESH)

    lower = (up < zh).astype(jnp.int32) + (down < zh).astype(jnp.int32)

    def block(q, b, a):
        dy, dx = (b, a) if BY_X[q] else (a, b)
        start = ((zh + STEPS[q]) % 4) * 16 + ((y + dy) % 4) * 4 + (x + dx) % 4
        return hidden.at[:, pl.ds(pl.multiple_of(start * 128, 128), 128)]

    def place(q, b, a):
        return hbuf.at[q, pl.ds(pl.multiple_of(a * 128, 128), 128), pl.ds(pl.multiple_of(b * 128, 128), 128)]

    mine = pl.ds(pl.multiple_of(rep * 16, 16), 16)
    shared = [
        pltpu.make_async_copy(cotan, cbuf.at[0, pl.ds(0, 128)], local.at[4]),
        pltpu.make_async_copy(cotan, cbuf.at[1, pl.ds(0, 128)], local.at[7]),
        pltpu.make_async_copy(frag.at[0, mine], dpart.at[0], local.at[5]),
        pltpu.make_async_copy(anchor.at[mine], danchor, local.at[6]),
    ]
    for copy in shared:
        copy.start()
    for q in range(4):
        @pl.loop(0, 4)
        def _(b):
            pltpu.make_async_copy(block(q, b, 0), place(q, b, 0), local.at[q]).start()

    pl.semaphore_wait(barrier, 6 + rep + lower)

    @pl.loop(0, rep)
    def _(r):
        pl.semaphore_signal(ready.at[0], inc=1, device_id=(r, row), device_id_type=MESH)

    for dz, at in ((1, up), (3, down)):
        @pl.when(at < zh)
        def _():
            pl.semaphore_signal(ready.at[1], inc=1, device_id=along_z(dz), device_id_type=MESH)

    for d in (1, 3, 2):
        send(cotan, cbuf.at[0, pl.ds(d * 128, 128)], csend.at[0], crecv.at[0], along_x(d))
        send(cotan, cbuf.at[1, pl.ds(d * 128, 128)], csend.at[1], crecv.at[1], along_y(d))

    def features(q):
        @pl.loop(0, 12)
        def _(k):
            a, b = 1 + k // 4, k % 4
            device = along_x(a) if BY_X[q] else along_y(a)
            send(block(q, b, a), place(q, b, a), hsend.at[q], hrecv.at[q], device)

    def sent(q):
        wait(hbuf.at[q, pl.ds(128, 384)], hsend.at[q])

    features(0)
    features(1)

    @pl.when(rep < 7)
    def _():
        pl.semaphore_wait(ready.at[0], 7 - rep)

    @pl.loop(1, 8)
    def _(j):
        rows = pl.ds(pl.multiple_of(((rep + j) % 8) * 16, 16), 16)
        send(frag.at[0, rows], dpart.at[j], dsend.at[0], drecv.at[0], other(j))

    def encode(value, codes, tops):
        top = jnp.maximum(jnp.max(jnp.abs(value), axis=0, keepdims=True), 1e-30)
        codes[...] = jnp.round(value * (32767.0 / top)).astype(jnp.int32).astype(jnp.int16)
        for c in range(top.shape[1] // 128):
            tops[pl.ds(c, 1)] = top[:, c * 128 : c * 128 + 128]

    def decode(codes, tops):
        top = jnp.concatenate([tops[pl.ds(c, 1)] for c in range(tops.shape[0])], axis=1)
        return codes[...].astype(jnp.int32).astype(jnp.float32) * (top * (1.0 / 32767.0))

    def product(q, b):
        left = hbuf[q, :, pl.ds(pl.multiple_of(b * 128, 128), 128)]
        right = cbuf[0 if BY_X[q] else 1]
        return lax.dot_general(left, right, (((0,), (0,)), ((), ())), preferred_element_type=jnp.float32)

    def scatter(q):
        wait(hbuf.at[q, pl.ds(0, 128)], local.at[q])
        wait(hbuf.at[q, pl.ds(128, 384)], hrecv.at[q])

        @pl.loop(1, 4)
        def _(b):
            encode(product(q, b), ycode.at[q, b - 1], ygain.at[q, b - 1])
            device = along_y(b) if BY_X[q] else along_x(b)
            send(ycode.at[q, b - 1], yrecode.at[q, b - 1], ysend.at[0, q], yrecv.at[0, q], device)
            send(ygain.at[q, b - 1], yregain.at[q, b - 1], ysend.at[1, q], yrecv.at[1, q], device)

        part[q] = product(q, 0)

    def gather(q):
        wait(yrecode.at[q], yrecv.at[0, q])
        wait(yregain.at[q], yrecv.at[1, q])
        total = part[q]
        for d in range(3):
            total += decode(yrecode.at[q, d], yregain.at[q, d])
        part[q] = total

    first, second = pl.ds(0, 256), pl.ds(256, 256)

    def pass_on(m, value, dz):
        encode(value, code.at[m], gain.at[m])
        send(code.at[m], recode.at[m], zsend.at[m], zrecv.at[m], along_z(dz))
        send(gain.at[m], regain.at[m], zsend.at[6 + m], zrecv.at[6 + m], along_z(dz))

    def received(m):
        wait(recode.at[m], zrecv.at[m])
        wait(regain.at[m], zrecv.at[6 + m])
        return decode(recode.at[m], regain.at[m])

    shared[0].wait()
    wait(cbuf.at[0, pl.ds(128, 384)], crecv.at[0])
    scatter(0)
    shared[1].wait()
    wait(cbuf.at[1, pl.ds(128, 384)], crecv.at[1])
    scatter(1)

    shared[2].wait()
    shared[3].wait()
    wait(dpart.at[pl.ds(1, 7)], drecv.at[0])
    total = danchor[...] - dpart[0].astype(jnp.float32)
    for j in range(1, 8):
        total += danchor[...] - dpart[j].astype(jnp.float32)
    dsum[mine] = total / 8

    for j in (2, 4, 6):
        send(dsum.at[mine], dsum.at[mine], dsend.at[1], drecv.at[1], other(j))
    sibling = (rep + 1 - 2 * (rep % 2), row)
    send(dsum.at[mine], dsum.at[mine], dsend.at[2], drecv.at[2], sibling)

    sent(0)
    features(3)
    sent(1)
    features(2)
    gather(0)

    @pl.when(lower < 2)
    def _():
        pl.semaphore_wait(ready.at[1], 2 - lower)

    pass_on(0, part[0, :, first], 1)
    pass_on(1, part[0, :, second], 3)
    gather(1)
    pass_on(2, part[1, :, second], 1)
    scatter(2)
    scatter(3)
    pass_on(4, part[1, :, first] + received(0), 1)
    gather(2)
    pass_on(3, part[2, :, first], 3)
    pass_on(5, part[2, :, second] + received(1), 3)
    wait(dsum.at[pl.ds(0, 48)], drecv.at[1])
    for j in (2, 4, 6):
        there = pl.ds(pl.multiple_of(((rep + j) % 8) * 16, 16), 16)
        send(dsum.at[there], dsum.at[there], dsend.at[3], drecv.at[3], sibling)
    gather(3)

    wait(dsum.at[pl.ds(0, 16)], drecv.at[2])
    wait(dsum.at[pl.ds(0, 48)], drecv.at[3])
    delta[...] = dsum[...]
    part[3, :, second] += received(2)
    part[3, :, first] += received(3)
    grad[:, first] = part[3, :, first] + received(4)
    grad[:, second] = part[3, :, second] + received(5)

    for q in range(4):
        if q > 1:
            sent(q)
        wait(ycode.at[q], ysend.at[0, q])
        wait(ygain.at[q], ysend.at[1, q])
    wait(cbuf.at[0, pl.ds(128, 384)], csend.at[0])
    wait(cbuf.at[1, pl.ds(128, 384)], csend.at[1])
    for m in range(6):
        wait(code.at[m], zsend.at[m])
        wait(gain.at[m], zsend.at[6 + m])
    wait(dpart.at[pl.ds(1, 7)], dsend.at[0])
    wait(dsum.at[pl.ds(0, 48)], dsend.at[1])
    wait(dsum.at[pl.ds(0, 16)], dsend.at[2])
    wait(dsum.at[pl.ds(0, 48)], dsend.at[3])


def update(
    corr_one, corr_two, grad, delta, weight, first, second, anchor, momentum,
    new_weight, new_first, new_second, new_anchor, new_momentum,
):
    slope = grad[...]
    moment = 0.9 * first[0] + 0.1 * slope
    square = 0.999 * second[0] + 0.001 * slope * slope
    new_first[0] = moment
    new_second[0] = square
    step = moment / corr_one[0] / (jnp.sqrt(square / corr_two[0]) + 1e-08)
    new_weight[0] = weight[0] - 0.01 * (step + 0.1 * weight[0])
    change = delta[...]
    speed = 0.9 * momentum[...] + change
    new_momentum[...] = speed
    new_anchor[...] = anchor[...] - 0.7 * (change + 0.9 * speed)


def body(
    hidden,
    key_cotangent,
    key_weight,
    first_moment,
    second_moment,
    step_index,
    anchor,
    outer_momentum,
    replica_fragment,
):
    dma = pltpu.SemaphoreType.DMA
    grad, delta = pl.pallas_call(
        exchange,
        out_shape=[jax.ShapeDtypeStruct((128, 512), jnp.float32)] * 2,
        in_specs=[pl.BlockSpec(memory_space=pl.ANY)] * 4,
        out_specs=[pl.BlockSpec(memory_space=pltpu.VMEM)] * 2,
        scratch_shapes=[
            pltpu.VMEM((4, 512, 512), jnp.bfloat16),
            pltpu.VMEM((2, 512, 512), jnp.bfloat16),
            pltpu.VMEM((4, 3, 128, 512), jnp.int16),
            pltpu.VMEM((4, 3, 4, 128), jnp.float32),
            pltpu.VMEM((4, 3, 128, 512), jnp.int16),
            pltpu.VMEM((4, 3, 4, 128), jnp.float32),
            pltpu.VMEM((4, 128, 512), jnp.float32),
            pltpu.VMEM((6, 128, 256), jnp.int16),
            pltpu.VMEM((6, 2, 128), jnp.float32),
            pltpu.VMEM((6, 128, 256), jnp.int16),
            pltpu.VMEM((6, 2, 128), jnp.float32),
            pltpu.VMEM((8, 16, 512), jnp.bfloat16),
            pltpu.VMEM((16, 512), jnp.float32),
            pltpu.VMEM((128, 512), jnp.float32),
            dma((8,)), dma((4,)), dma((4,)), dma((2,)), dma((2,)), dma((2, 4)), dma((2, 4)),
            dma((12,)), dma((12,)), dma((4,)), dma((4,)), pltpu.SemaphoreType.REGULAR((2,)),
        ],
        compiler_params=pltpu.CompilerParams(
            collective_id=0, has_side_effects=True, vmem_limit_bytes=60 * 1024 * 1024
        ),
        cost_estimate=pl.CostEstimate(flops=2 * 2048 * 512 * 512, bytes_accessed=8 << 20, transcendentals=0),
        name="exchange",
    )(hidden, key_cotangent, replica_fragment, anchor)
    steps = step_index.astype(jnp.float32)
    corr_one = 1.0 - jnp.power(jnp.float32(0.9), steps)
    corr_two = 1.0 - jnp.power(jnp.float32(0.999), steps)
    parts = 2
    scalar = pl.BlockSpec(memory_space=pltpu.SMEM)
    flat = pl.BlockSpec((128 // parts, 512), lambda i: (i, 0))
    deep = pl.BlockSpec((1, 128 // parts, 512), lambda i: (0, i, 0))
    return pl.pallas_call(
        update,
        grid=(parts,),
        out_shape=[jax.ShapeDtypeStruct((1, 128, 512), jnp.float32)] * 3 + [jax.ShapeDtypeStruct((128, 512), jnp.float32)] * 2,
        in_specs=[scalar] * 2 + [flat] * 2 + [deep] * 3 + [flat] * 2,
        out_specs=[deep] * 3 + [flat] * 2,
        name="update",
    )(corr_one[None], corr_two[None], grad, delta, key_weight, first_moment, second_moment, anchor, outer_momentum)


def solution(mesh):
    return jax.shard_map(
        body,
        mesh=mesh,
        in_specs=(
            P(("replica", "fsdp"), None),
            P(("replica", "fsdp"), None),
            P("replica", "fsdp", None),
            P("replica", "fsdp", None),
            P("replica", "fsdp", None),
            P(),
            P("fsdp", None),
            P("fsdp", None),
            P("replica", "fsdp", None),
        ),
        out_specs=(
            P("replica", "fsdp", None),
            P("replica", "fsdp", None),
            P("replica", "fsdp", None),
            P("fsdp", None),
            P("fsdp", None),
        ),
        check_vma=False,
    )
```

```python
import functools

import jax
import jax.numpy as jnp
from jax import lax
from jax.experimental import pallas as pl
from jax.experimental.pallas import tpu as pltpu
from jax.sharding import PartitionSpec as P

MESH = pl.DeviceIdType.MESH
STEPS = (2, 1, 3, 0)
BY_X = (True, False, True, False)


def exchange(
    hidden, cotan, frag, anchor, grad, delta,
    hbuf, cbuf, ycode, ygain, yrecode, yregain, part, code, gain, recode, regain, dpart, danchor, dsum,
    local, hsend, hrecv, csend, crecv, ysend, yrecv, zsend, zrecv, dsend, drecv, ready,
):
    rep = lax.axis_index("replica")
    row = lax.axis_index("fsdp")
    zh, y, x = row // 16, (row // 4) % 4, row % 4

    def along_x(dx):
        return (rep, zh * 16 + y * 4 + (x + dx) % 4)

    def along_y(dy):
        return (rep, zh * 16 + ((y + dy) % 4) * 4 + x)

    def along_z(dz):
        return (rep, ((zh + dz) % 4) * 16 + y * 4 + x)

    def other(j):
        return ((rep + j) % 8, row)

    def send(src, dst, ssem, rsem, device):
        pltpu.make_async_remote_copy(
            src_ref=src, dst_ref=dst, send_sem=ssem, recv_sem=rsem, device_id=device, device_id_type=MESH
        ).start()

    def wait(ref, sem):
        pltpu.make_async_copy(ref, ref, sem).wait()

    up, down = (zh + 1) % 4, (zh + 3) % 4
    barrier = pltpu.get_barrier_semaphore()
    for d in (1, 2, 3):
        pl.semaphore_signal(barrier, inc=1, device_id=along_x(d), device_id_type=MESH)
        pl.semaphore_signal(barrier, inc=1, device_id=along_y(d), device_id_type=MESH)

    @pl.loop(rep + 1, 8)
    def _(r):
        pl.semaphore_signal(barrier, inc=1, device_id=(r, row), device_id_type=MESH)

    for dz, at in ((1, up), (3, down)):
        @pl.when(at > zh)
        def _():
            pl.semaphore_signal(barrier, inc=1, device_id=along_z(dz), device_id_type=MESH)

    lower = (up < zh).astype(jnp.int32) + (down < zh).astype(jnp.int32)

    def block(q, b, a):
        dy, dx = (b, a) if BY_X[q] else (a, b)
        start = ((zh + STEPS[q]) % 4) * 16 + ((y + dy) % 4) * 4 + (x + dx) % 4
        return hidden.at[:, pl.ds(pl.multiple_of(start * 128, 128), 128)]

    def place(q, b, a):
        return hbuf.at[q, pl.ds(pl.multiple_of(a * 128, 128), 128), pl.ds(pl.multiple_of(b * 128, 128), 128)]

    mine = pl.ds(pl.multiple_of(rep * 16, 16), 16)
    shared = [
        pltpu.make_async_copy(cotan, cbuf.at[0, pl.ds(0, 128)], local.at[4]),
        pltpu.make_async_copy(cotan, cbuf.at[1, pl.ds(0, 128)], local.at[7]),
        pltpu.make_async_copy(frag.at[0, mine], dpart.at[0], local.at[5]),
        pltpu.make_async_copy(anchor.at[mine], danchor, local.at[6]),
    ]
    for copy in shared:
        copy.start()
    for q in range(4):
        @pl.loop(0, 4)
        def _(b):
            pltpu.make_async_copy(block(q, b, 0), place(q, b, 0), local.at[q]).start()

    pl.semaphore_wait(barrier, 6 + rep + lower)

    @pl.loop(0, rep)
    def _(r):
        pl.semaphore_signal(ready.at[0], inc=1, device_id=(r, row), device_id_type=MESH)

    for dz, at in ((1, up), (3, down)):
        @pl.when(at < zh)
        def _():
            pl.semaphore_signal(ready.at[1], inc=1, device_id=along_z(dz), device_id_type=MESH)

    for d in (1, 3, 2):
        send(cotan, cbuf.at[0, pl.ds(d * 128, 128)], csend.at[0], crecv.at[0], along_x(d))
        send(cotan, cbuf.at[1, pl.ds(d * 128, 128)], csend.at[1], crecv.at[1], along_y(d))

    def features(q):
        @pl.loop(0, 12)
        def _(k):
            a, b = 1 + k // 4, k % 4
            device = along_x(a) if BY_X[q] else along_y(a)
            send(block(q, b, a), place(q, b, a), hsend.at[q], hrecv.at[q], device)

    def sent(q):
        wait(hbuf.at[q, pl.ds(128, 384)], hsend.at[q])

    features(0)
    features(1)

    @pl.when(rep < 7)
    def _():
        pl.semaphore_wait(ready.at[0], 7 - rep)

    @pl.loop(1, 8)
    def _(j):
        rows = pl.ds(pl.multiple_of(((rep + j) % 8) * 16, 16), 16)
        send(frag.at[0, rows], dpart.at[j], dsend.at[0], drecv.at[0], other(j))

    def encode(value, codes, tops):
        top = jnp.maximum(jnp.max(jnp.abs(value), axis=0, keepdims=True), 1e-30)
        codes[...] = jnp.round(value * (32767.0 / top)).astype(jnp.int32).astype(jnp.int16)
        for c in range(top.shape[1] // 128):
            tops[pl.ds(c, 1)] = top[:, c * 128 : c * 128 + 128]

    def decode(codes, tops):
        top = jnp.concatenate([tops[pl.ds(c, 1)] for c in range(tops.shape[0])], axis=1)
        return codes[...].astype(jnp.int32).astype(jnp.float32) * (top * (1.0 / 32767.0))

    def product(q, b):
        left = hbuf[q, :, pl.ds(pl.multiple_of(b * 128, 128), 128)]
        right = cbuf[0 if BY_X[q] else 1]
        return lax.dot_general(left, right, (((0,), (0,)), ((), ())), preferred_element_type=jnp.float32)

    def scatter(q):
        wait(hbuf.at[q, pl.ds(0, 128)], local.at[q])
        wait(hbuf.at[q, pl.ds(128, 384)], hrecv.at[q])

        @pl.loop(1, 4)
        def _(b):
            encode(product(q, b), ycode.at[q, b - 1], ygain.at[q, b - 1])
            device = along_y(b) if BY_X[q] else along_x(b)
            send(ycode.at[q, b - 1], yrecode.at[q, b - 1], ysend.at[0, q], yrecv.at[0, q], device)
            send(ygain.at[q, b - 1], yregain.at[q, b - 1], ysend.at[1, q], yrecv.at[1, q], device)

        part[q] = product(q, 0)

    def gather(q):
        wait(yrecode.at[q], yrecv.at[0, q])
        wait(yregain.at[q], yrecv.at[1, q])
        total = part[q]
        for d in range(3):
            total += decode(yrecode.at[q, d], yregain.at[q, d])
        part[q] = total

    first, second = pl.ds(0, 256), pl.ds(256, 256)

    def pass_on(m, value, dz):
        encode(value, code.at[m], gain.at[m])
        send(code.at[m], recode.at[m], zsend.at[m], zrecv.at[m], along_z(dz))
        send(gain.at[m], regain.at[m], zsend.at[6 + m], zrecv.at[6 + m], along_z(dz))

    def received(m):
        wait(recode.at[m], zrecv.at[m])
        wait(regain.at[m], zrecv.at[6 + m])
        return decode(recode.at[m], regain.at[m])

    sent(0)
    features(2)
    shared[0].wait()
    wait(cbuf.at[0, pl.ds(128, 384)], crecv.at[0])
    scatter(0)
    shared[1].wait()
    wait(cbuf.at[1, pl.ds(128, 384)], crecv.at[1])
    scatter(1)

    shared[2].wait()
    shared[3].wait()
    wait(dpart.at[pl.ds(1, 7)], drecv.at[0])
    total = danchor[...] - dpart[0].astype(jnp.float32)
    for j in range(1, 8):
        total += danchor[...] - dpart[j].astype(jnp.float32)
    dsum[mine] = total / 8

    for j in (2, 4, 6):
        send(dsum.at[mine], dsum.at[mine], dsend.at[1], drecv.at[1], other(j))
    sibling = (rep + 1 - 2 * (rep % 2), row)
    send(dsum.at[mine], dsum.at[mine], dsend.at[2], drecv.at[2], sibling)

    gather(0)

    @pl.when(lower < 2)
    def _():
        pl.semaphore_wait(ready.at[1], 2 - lower)

    pass_on(0, part[0, :, first], 1)
    pass_on(1, part[0, :, second], 3)
    gather(1)
    pass_on(2, part[1, :, second], 1)
    scatter(2)
    sent(1)
    features(3)
    pass_on(4, part[1, :, first] + received(0), 1)
    gather(2)
    pass_on(3, part[2, :, first], 3)
    pass_on(5, part[2, :, second] + received(1), 3)
    scatter(3)
    wait(dsum.at[pl.ds(0, 48)], drecv.at[1])
    for j in (2, 4, 6):
        there = pl.ds(pl.multiple_of(((rep + j) % 8) * 16, 16), 16)
        send(dsum.at[there], dsum.at[there], dsend.at[3], drecv.at[3], sibling)
    gather(3)

    wait(dsum.at[pl.ds(0, 16)], drecv.at[2])
    wait(dsum.at[pl.ds(0, 48)], drecv.at[3])
    delta[...] = dsum[...]
    part[3, :, second] += received(2)
    part[3, :, first] += received(3)
    grad[:, first] = part[3, :, first] + received(4)
    grad[:, second] = part[3, :, second] + received(5)

    for q in range(4):
        if q > 1:
            sent(q)
        wait(ycode.at[q], ysend.at[0, q])
        wait(ygain.at[q], ysend.at[1, q])
    wait(cbuf.at[0, pl.ds(128, 384)], csend.at[0])
    wait(cbuf.at[1, pl.ds(128, 384)], csend.at[1])
    for m in range(6):
        wait(code.at[m], zsend.at[m])
        wait(gain.at[m], zsend.at[6 + m])
    wait(dpart.at[pl.ds(1, 7)], dsend.at[0])
    wait(dsum.at[pl.ds(0, 48)], dsend.at[1])
    wait(dsum.at[pl.ds(0, 16)], dsend.at[2])
    wait(dsum.at[pl.ds(0, 48)], dsend.at[3])


def update(
    corr_one, corr_two, grad, delta, weight, first, second, anchor, momentum,
    new_weight, new_first, new_second, new_anchor, new_momentum,
):
    slope = grad[...]
    moment = 0.9 * first[0] + 0.1 * slope
    square = 0.999 * second[0] + 0.001 * slope * slope
    new_first[0] = moment
    new_second[0] = square
    step = moment / corr_one[0] / (jnp.sqrt(square / corr_two[0]) + 1e-08)
    new_weight[0] = weight[0] - 0.01 * (step + 0.1 * weight[0])
    change = delta[...]
    speed = 0.9 * momentum[...] + change
    new_momentum[...] = speed
    new_anchor[...] = anchor[...] - 0.7 * (change + 0.9 * speed)


def body(
    hidden,
    key_cotangent,
    key_weight,
    first_moment,
    second_moment,
    step_index,
    anchor,
    outer_momentum,
    replica_fragment,
):
    dma = pltpu.SemaphoreType.DMA
    grad, delta = pl.pallas_call(
        exchange,
        out_shape=[jax.ShapeDtypeStruct((128, 512), jnp.float32)] * 2,
        in_specs=[pl.BlockSpec(memory_space=pl.ANY)] * 4,
        out_specs=[pl.BlockSpec(memory_space=pltpu.VMEM)] * 2,
        scratch_shapes=[
            pltpu.VMEM((4, 512, 512), jnp.bfloat16),
            pltpu.VMEM((2, 512, 512), jnp.bfloat16),
            pltpu.VMEM((4, 3, 128, 512), jnp.int16),
            pltpu.VMEM((4, 3, 4, 128), jnp.float32),
            pltpu.VMEM((4, 3, 128, 512), jnp.int16),
            pltpu.VMEM((4, 3, 4, 128), jnp.float32),
            pltpu.VMEM((4, 128, 512), jnp.float32),
            pltpu.VMEM((6, 128, 256), jnp.int16),
            pltpu.VMEM((6, 2, 128), jnp.float32),
            pltpu.VMEM((6, 128, 256), jnp.int16),
            pltpu.VMEM((6, 2, 128), jnp.float32),
            pltpu.VMEM((8, 16, 512), jnp.bfloat16),
            pltpu.VMEM((16, 512), jnp.float32),
            pltpu.VMEM((128, 512), jnp.float32),
            dma((8,)), dma((4,)), dma((4,)), dma((2,)), dma((2,)), dma((2, 4)), dma((2, 4)),
            dma((12,)), dma((12,)), dma((4,)), dma((4,)), pltpu.SemaphoreType.REGULAR((2,)),
        ],
        compiler_params=pltpu.CompilerParams(
            collective_id=0, has_side_effects=True, vmem_limit_bytes=60 * 1024 * 1024
        ),
        cost_estimate=pl.CostEstimate(flops=2 * 2048 * 512 * 512, bytes_accessed=8 << 20, transcendentals=0),
        name="exchange",
    )(hidden, key_cotangent, replica_fragment, anchor)
    steps = step_index.astype(jnp.float32)
    corr_one = 1.0 - jnp.power(jnp.float32(0.9), steps)
    corr_two = 1.0 - jnp.power(jnp.float32(0.999), steps)
    parts = 2
    scalar = pl.BlockSpec(memory_space=pltpu.SMEM)
    flat = pl.BlockSpec((128 // parts, 512), lambda i: (i, 0))
    deep = pl.BlockSpec((1, 128 // parts, 512), lambda i: (0, i, 0))
    return pl.pallas_call(
        update,
        grid=(parts,),
        out_shape=[jax.ShapeDtypeStruct((1, 128, 512), jnp.float32)] * 3 + [jax.ShapeDtypeStruct((128, 512), jnp.float32)] * 2,
        in_specs=[scalar] * 2 + [flat] * 2 + [deep] * 3 + [flat] * 2,
        out_specs=[deep] * 3 + [flat] * 2,
        name="update",
    )(corr_one[None], corr_two[None], grad, delta, key_weight, first_moment, second_moment, anchor, outer_momentum)


def solution(mesh):
    return jax.shard_map(
        body,
        mesh=mesh,
        in_specs=(
            P(("replica", "fsdp"), None),
            P(("replica", "fsdp"), None),
            P("replica", "fsdp", None),
            P("replica", "fsdp", None),
            P("replica", "fsdp", None),
            P(),
            P("fsdp", None),
            P("fsdp", None),
            P("replica", "fsdp", None),
        ),
        out_specs=(
            P("replica", "fsdp", None),
            P("replica", "fsdp", None),
            P("replica", "fsdp", None),
            P("fsdp", None),
            P("fsdp", None),
        ),
        check_vma=False,
    )
```

```python
import functools

import jax
import jax.numpy as jnp
from jax import lax
from jax.experimental import pallas as pl
from jax.experimental.pallas import tpu as pltpu
from jax.sharding import PartitionSpec as P

MESH = pl.DeviceIdType.MESH
STEPS = (2, 1, 3, 0)
BY_X = (True, False, True, False)


def exchange(
    hidden, cotan, frag, anchor, grad, delta,
    hbuf, cbuf, ycode, ygain, yrecode, yregain, part, code, gain, recode, regain, dpart, danchor, dsum,
    local, hsend, hrecv, csend, crecv, ysend, yrecv, zsend, zrecv, dsend, drecv, ready,
):
    rep = lax.axis_index("replica")
    row = lax.axis_index("fsdp")
    zh, y, x = row // 16, (row // 4) % 4, row % 4

    def along_x(dx):
        return (rep, zh * 16 + y * 4 + (x + dx) % 4)

    def along_y(dy):
        return (rep, zh * 16 + ((y + dy) % 4) * 4 + x)

    def along_z(dz):
        return (rep, ((zh + dz) % 4) * 16 + y * 4 + x)

    def other(j):
        return ((rep + j) % 8, row)

    def send(src, dst, ssem, rsem, device):
        pltpu.make_async_remote_copy(
            src_ref=src, dst_ref=dst, send_sem=ssem, recv_sem=rsem, device_id=device, device_id_type=MESH
        ).start()

    def wait(ref, sem):
        pltpu.make_async_copy(ref, ref, sem).wait()

    up, down = (zh + 1) % 4, (zh + 3) % 4
    barrier = pltpu.get_barrier_semaphore()
    for d in (1, 2, 3):
        pl.semaphore_signal(barrier, inc=1, device_id=along_x(d), device_id_type=MESH)
        pl.semaphore_signal(barrier, inc=1, device_id=along_y(d), device_id_type=MESH)

    @pl.loop(rep + 1, 8)
    def _(r):
        pl.semaphore_signal(barrier, inc=1, device_id=(r, row), device_id_type=MESH)

    for dz, at in ((1, up), (3, down)):
        @pl.when(at > zh)
        def _():
            pl.semaphore_signal(barrier, inc=1, device_id=along_z(dz), device_id_type=MESH)

    lower = (up < zh).astype(jnp.int32) + (down < zh).astype(jnp.int32)

    def block(q, b, a):
        dy, dx = (b, a) if BY_X[q] else (a, b)
        start = ((zh + STEPS[q]) % 4) * 16 + ((y + dy) % 4) * 4 + (x + dx) % 4
        return hidden.at[:, pl.ds(pl.multiple_of(start * 128, 128), 128)]

    def place(q, b, a):
        return hbuf.at[q, pl.ds(pl.multiple_of(a * 128, 128), 128), pl.ds(pl.multiple_of(b * 128, 128), 128)]

    mine = pl.ds(pl.multiple_of(rep * 16, 16), 16)
    shared = [
        pltpu.make_async_copy(cotan, cbuf.at[0, pl.ds(0, 128)], local.at[4]),
        pltpu.make_async_copy(cotan, cbuf.at[1, pl.ds(0, 128)], local.at[7]),
        pltpu.make_async_copy(frag.at[0, mine], dpart.at[0], local.at[5]),
        pltpu.make_async_copy(anchor.at[mine], danchor, local.at[6]),
    ]
    for copy in shared:
        copy.start()
    for q in range(4):
        @pl.loop(0, 4)
        def _(b):
            pltpu.make_async_copy(block(q, b, 0), place(q, b, 0), local.at[q]).start()

    pl.semaphore_wait(barrier, 6 + rep + lower)

    @pl.loop(0, rep)
    def _(r):
        pl.semaphore_signal(ready.at[0], inc=1, device_id=(r, row), device_id_type=MESH)

    for dz, at in ((1, up), (3, down)):
        @pl.when(at < zh)
        def _():
            pl.semaphore_signal(ready.at[1], inc=1, device_id=along_z(dz), device_id_type=MESH)

    for d in (2, 1, 3):
        send(cotan, cbuf.at[0, pl.ds(d * 128, 128)], csend.at[0], crecv.at[0], along_x(d))
        send(cotan, cbuf.at[1, pl.ds(d * 128, 128)], csend.at[1], crecv.at[1], along_y(d))

    def features(q):
        @pl.loop(0, 12)
        def _(k):
            a, b = 1 + (k // 4 + 1) % 3, k % 4
            device = along_x(a) if BY_X[q] else along_y(a)
            send(block(q, b, a), place(q, b, a), hsend.at[q], hrecv.at[q], device)

    def sent(q):
        wait(hbuf.at[q, pl.ds(128, 384)], hsend.at[q])

    features(0)
    features(1)

    @pl.when(rep < 7)
    def _():
        pl.semaphore_wait(ready.at[0], 7 - rep)

    @pl.loop(1, 8)
    def _(j):
        rows = pl.ds(pl.multiple_of(((rep + j) % 8) * 16, 16), 16)
        send(frag.at[0, rows], dpart.at[j], dsend.at[0], drecv.at[0], other(j))

    def encode(value, codes, tops):
        top = jnp.maximum(jnp.max(jnp.abs(value), axis=0, keepdims=True), 1e-30)
        codes[...] = jnp.round(value * (32767.0 / top)).astype(jnp.int32).astype(jnp.int16)
        for c in range(top.shape[1] // 128):
            tops[pl.ds(c, 1)] = top[:, c * 128 : c * 128 + 128]

    def decode(codes, tops):
        top = jnp.concatenate([tops[pl.ds(c, 1)] for c in range(tops.shape[0])], axis=1)
        return codes[...].astype(jnp.int32).astype(jnp.float32) * (top * (1.0 / 32767.0))

    def product(q, b):
        left = hbuf[q, :, pl.ds(pl.multiple_of(b * 128, 128), 128)]
        right = cbuf[0 if BY_X[q] else 1]
        return lax.dot_general(left, right, (((0,), (0,)), ((), ())), preferred_element_type=jnp.float32)

    def scatter(q):
        wait(hbuf.at[q, pl.ds(0, 128)], local.at[q])
        wait(hbuf.at[q, pl.ds(128, 384)], hrecv.at[q])

        @pl.loop(0, 3)
        def _(i):
            b = 1 + (i + 1) % 3
            encode(product(q, b), ycode.at[q, b - 1], ygain.at[q, b - 1])
            device = along_y(b) if BY_X[q] else along_x(b)
            send(ycode.at[q, b - 1], yrecode.at[q, b - 1], ysend.at[0, q], yrecv.at[0, q], device)
            send(ygain.at[q, b - 1], yregain.at[q, b - 1], ysend.at[1, q], yrecv.at[1, q], device)

        part[q] = product(q, 0)

    def gather(q):
        wait(yrecode.at[q], yrecv.at[0, q])
        wait(yregain.at[q], yrecv.at[1, q])
        total = part[q]
        for d in range(3):
            total += decode(yrecode.at[q, d], yregain.at[q, d])
        part[q] = total

    first, second = pl.ds(0, 256), pl.ds(256, 256)

    def pass_on(m, value, dz):
        encode(value, code.at[m], gain.at[m])
        send(code.at[m], recode.at[m], zsend.at[m], zrecv.at[m], along_z(dz))
        send(gain.at[m], regain.at[m], zsend.at[6 + m], zrecv.at[6 + m], along_z(dz))

    def received(m):
        wait(recode.at[m], zrecv.at[m])
        wait(regain.at[m], zrecv.at[6 + m])
        return decode(recode.at[m], regain.at[m])

    sent(0)
    features(2)
    shared[0].wait()
    wait(cbuf.at[0, pl.ds(128, 384)], crecv.at[0])
    scatter(0)
    shared[1].wait()
    wait(cbuf.at[1, pl.ds(128, 384)], crecv.at[1])
    scatter(1)

    shared[2].wait()
    shared[3].wait()
    wait(dpart.at[pl.ds(1, 7)], drecv.at[0])
    total = danchor[...] - dpart[0].astype(jnp.float32)
    for j in range(1, 8):
        total += danchor[...] - dpart[j].astype(jnp.float32)
    dsum[mine] = total / 8

    for j in (2, 4, 6):
        send(dsum.at[mine], dsum.at[mine], dsend.at[1], drecv.at[1], other(j))
    sibling = (rep + 1 - 2 * (rep % 2), row)
    send(dsum.at[mine], dsum.at[mine], dsend.at[2], drecv.at[2], sibling)

    gather(0)

    @pl.when(lower < 2)
    def _():
        pl.semaphore_wait(ready.at[1], 2 - lower)

    pass_on(0, part[0, :, first], 1)
    pass_on(1, part[0, :, second], 3)
    gather(1)
    pass_on(2, part[1, :, second], 1)
    scatter(2)
    sent(1)
    features(3)
    pass_on(4, part[1, :, first] + received(0), 1)
    gather(2)
    pass_on(3, part[2, :, first], 3)
    pass_on(5, part[2, :, second] + received(1), 3)
    scatter(3)
    wait(dsum.at[pl.ds(0, 48)], drecv.at[1])
    for j in (2, 4, 6):
        there = pl.ds(pl.multiple_of(((rep + j) % 8) * 16, 16), 16)
        send(dsum.at[there], dsum.at[there], dsend.at[3], drecv.at[3], sibling)
    gather(3)

    wait(dsum.at[pl.ds(0, 16)], drecv.at[2])
    wait(dsum.at[pl.ds(0, 48)], drecv.at[3])
    delta[...] = dsum[...]
    part[3, :, second] += received(2)
    part[3, :, first] += received(3)
    grad[:, first] = part[3, :, first] + received(4)
    grad[:, second] = part[3, :, second] + received(5)

    for q in range(4):
        if q > 1:
            sent(q)
        wait(ycode.at[q], ysend.at[0, q])
        wait(ygain.at[q], ysend.at[1, q])
    wait(cbuf.at[0, pl.ds(128, 384)], csend.at[0])
    wait(cbuf.at[1, pl.ds(128, 384)], csend.at[1])
    for m in range(6):
        wait(code.at[m], zsend.at[m])
        wait(gain.at[m], zsend.at[6 + m])
    wait(dpart.at[pl.ds(1, 7)], dsend.at[0])
    wait(dsum.at[pl.ds(0, 48)], dsend.at[1])
    wait(dsum.at[pl.ds(0, 16)], dsend.at[2])
    wait(dsum.at[pl.ds(0, 48)], dsend.at[3])


def update(
    corr_one, corr_two, grad, delta, weight, first, second, anchor, momentum,
    new_weight, new_first, new_second, new_anchor, new_momentum,
):
    slope = grad[...]
    moment = 0.9 * first[0] + 0.1 * slope
    square = 0.999 * second[0] + 0.001 * slope * slope
    new_first[0] = moment
    new_second[0] = square
    step = moment / corr_one[0] / (jnp.sqrt(square / corr_two[0]) + 1e-08)
    new_weight[0] = weight[0] - 0.01 * (step + 0.1 * weight[0])
    change = delta[...]
    speed = 0.9 * momentum[...] + change
    new_momentum[...] = speed
    new_anchor[...] = anchor[...] - 0.7 * (change + 0.9 * speed)


def body(
    hidden,
    key_cotangent,
    key_weight,
    first_moment,
    second_moment,
    step_index,
    anchor,
    outer_momentum,
    replica_fragment,
):
    dma = pltpu.SemaphoreType.DMA
    grad, delta = pl.pallas_call(
        exchange,
        out_shape=[jax.ShapeDtypeStruct((128, 512), jnp.float32)] * 2,
        in_specs=[pl.BlockSpec(memory_space=pl.ANY)] * 4,
        out_specs=[pl.BlockSpec(memory_space=pltpu.VMEM)] * 2,
        scratch_shapes=[
            pltpu.VMEM((4, 512, 512), jnp.bfloat16),
            pltpu.VMEM((2, 512, 512), jnp.bfloat16),
            pltpu.VMEM((4, 3, 128, 512), jnp.int16),
            pltpu.VMEM((4, 3, 4, 128), jnp.float32),
            pltpu.VMEM((4, 3, 128, 512), jnp.int16),
            pltpu.VMEM((4, 3, 4, 128), jnp.float32),
            pltpu.VMEM((4, 128, 512), jnp.float32),
            pltpu.VMEM((6, 128, 256), jnp.int16),
            pltpu.VMEM((6, 2, 128), jnp.float32),
            pltpu.VMEM((6, 128, 256), jnp.int16),
            pltpu.VMEM((6, 2, 128), jnp.float32),
            pltpu.VMEM((8, 16, 512), jnp.bfloat16),
            pltpu.VMEM((16, 512), jnp.float32),
            pltpu.VMEM((128, 512), jnp.float32),
            dma((8,)), dma((4,)), dma((4,)), dma((2,)), dma((2,)), dma((2, 4)), dma((2, 4)),
            dma((12,)), dma((12,)), dma((4,)), dma((4,)), pltpu.SemaphoreType.REGULAR((2,)),
        ],
        compiler_params=pltpu.CompilerParams(
            collective_id=0, has_side_effects=True, vmem_limit_bytes=60 * 1024 * 1024
        ),
        cost_estimate=pl.CostEstimate(flops=2 * 2048 * 512 * 512, bytes_accessed=8 << 20, transcendentals=0),
        name="exchange",
    )(hidden, key_cotangent, replica_fragment, anchor)
    steps = step_index.astype(jnp.float32)
    corr_one = 1.0 - jnp.power(jnp.float32(0.9), steps)
    corr_two = 1.0 - jnp.power(jnp.float32(0.999), steps)
    parts = 2
    scalar = pl.BlockSpec(memory_space=pltpu.SMEM)
    flat = pl.BlockSpec((128 // parts, 512), lambda i: (i, 0))
    deep = pl.BlockSpec((1, 128 // parts, 512), lambda i: (0, i, 0))
    return pl.pallas_call(
        update,
        grid=(parts,),
        out_shape=[jax.ShapeDtypeStruct((1, 128, 512), jnp.float32)] * 3 + [jax.ShapeDtypeStruct((128, 512), jnp.float32)] * 2,
        in_specs=[scalar] * 2 + [flat] * 2 + [deep] * 3 + [flat] * 2,
        out_specs=[deep] * 3 + [flat] * 2,
        name="update",
    )(corr_one[None], corr_two[None], grad, delta, key_weight, first_moment, second_moment, anchor, outer_momentum)


def solution(mesh):
    return jax.shard_map(
        body,
        mesh=mesh,
        in_specs=(
            P(("replica", "fsdp"), None),
            P(("replica", "fsdp"), None),
            P("replica", "fsdp", None),
            P("replica", "fsdp", None),
            P("replica", "fsdp", None),
            P(),
            P("fsdp", None),
            P("fsdp", None),
            P("replica", "fsdp", None),
        ),
        out_specs=(
            P("replica", "fsdp", None),
            P("replica", "fsdp", None),
            P("replica", "fsdp", None),
            P("fsdp", None),
            P("fsdp", None),
        ),
        check_vma=False,
    )
```
